32 devices in a mesh: groups: 2 (over y), adapter: 8 (over z, x), tensor: 2 (over core).
Axes of the slice: x: 2, y: 2, z: 4, core: 2. Of those that a mesh axis runs over, the one named last changes fastest.
Arguments:
- hidden: bfloat16 [128, 28672], P(('groups', 'adapter'), 'tensor'), parts along dimension 0, may hold values from -6 to 6
- row_adapter_index: int32 [128, 1], P('groups'), parts along dimension 0, may hold values from 0 to 7; in each aligned block of 64 rows (0 to 63, 64 to 127, ...) at most 16 rows name the same one
- down_matrix: bfloat16 [28672, 8192], P('tensor', 'adapter'), may hold values from -0.03125 to 0.03125
- adapter_input_factor: bfloat16 [8, 28672, 64], P('adapter', 'tensor'), may hold values from -0.03125 to 0.03125
- adapter_output_factor: bfloat16 [8, 64, 8192], P('adapter'), may hold values from -0.75 to 0.75
Outputs:
- mixed: bfloat16 [128, 8192], P('groups', ('adapter', 'tensor')), parts along dimension 0
The draws below stay inside these ranges and needn't reach their ends.
There are 2 independent parts, one for each index of `groups`. The reference program is written for one: setup_inputs(seed, part) draws one part's arguments, and reference() takes and returns one part's arrays. A program takes and returns all parts, laid end to end along the dimension named above; an argument that names none is the same for every part. Nothing has to cross between parts.
Inputs may be any that keep to these rules, and one draw needn't show every extreme that they name: `row_adapter_index`: each of the 8 adapters is named by 1 to 16 rows, a bound that some block reaches.
All inputs are finite; a program needn't handle non-finite values.
Results may differ from the reference program's by a relative error of at most 0.0049.
Values may be sent and summed in bfloat16 or wider, within the bound.
A program may use at most 128 MiB of HBM per device.

```python
import math
import jax
import jax.numpy as jnp
import numpy as np
from jax import lax

MODEL_WIDTH = 8192
HIDDEN_UNITS = 28672
ADAPTER_RANK = 64
ROWS = 64
ADAPTER_TOTAL = 8
CAP = 16


def shard_levels(key, extent, pieces, low, high):
    level = 1.0
    for position, blocks in pieces:
        heights = jax.random.uniform(jax.random.fold_in(jax.random.fold_in(key, 6), position), (blocks,), jnp.float32, low / len(pieces), high / len(pieces))
        level = level * jnp.repeat(jnp.exp(heights), extent[position] // blocks).reshape((-1,) + (1,) * (len(extent) - 1 - position))
    return level


def assign_block(rng, own, number, rows, amount, top, bound, slope):
    order = jax.random.permutation(rng, amount)
    packed, common = load_shares(amount, rows * top, bound, slope, True), load_shares(amount, rows * top, bound, slope, False)
    places = jnp.arange(amount)

    def named(sizes, offset_by):
        used = int((sizes > 0).sum())
        fixed = max(1, used // 4)
        shifted = fixed + (places - fixed + offset_by * (used - fixed)) % max(1, amount - fixed)
        return jnp.zeros((amount,), jnp.int32).at[order[jnp.where(places < fixed, places, shifted)]].set(jnp.asarray(sizes, jnp.int32))

    sizes = jnp.where(number % 4 == 0, named(packed, number // 4), named(common, number - number // 4 - 1))
    mixed = jax.random.permutation(jax.random.fold_in(own, 3), amount)
    source_of, receiver = mixed[0:amount // 2 * 2:2], mixed[1:amount // 2 * 2:2]
    slack = jnp.minimum(sizes[source_of] - 1, bound - sizes[receiver]) // 2
    slack = jnp.where((source_of == order[0]) | (receiver == order[0]) | (sizes[receiver] == 0), 0, jnp.maximum(slack, 0))
    shifted = jax.random.randint(jax.random.fold_in(own, 4), (amount // 2,), 0, 1 << 20) % (slack + 1)
    sizes = sizes.at[source_of].add(-shifted).at[receiver].add(shifted)
    labels = jnp.searchsorted(jnp.cumsum(sizes), jnp.arange(rows * top), side="right").astype(jnp.int32)
    table = labels.reshape(top, rows).T
    table = table[jax.random.permutation(jax.random.fold_in(own, 1), rows)]
    offset_by = jax.random.randint(jax.random.fold_in(own, 2), (rows, 1), 0, top)
    return jnp.take_along_axis(table, (jnp.arange(top)[None, :] + offset_by) % top, axis=1)


def load_shares(number_of, total, reach, slope, full):
    portions = [(1 << 20) // math.isqrt(standing ** slope) + 1 for standing in range(1, number_of + 1)]
    largest = reach if full else min(reach, max(-(-total // number_of), total * portions[0] // sum(portions)))
    least = 1 if total - largest >= number_of - 1 else 0
    counts, surplus = [largest] + [least] * (number_of - 1), total - largest - least * (number_of - 1)
    while surplus > 0:
        movable = [i for i in range(1, number_of) if counts[i] < largest] or [i for i in range(1, number_of) if counts[i] < reach]
        pool, left = sum([portions[i] for i in movable]), surplus
        for i in movable:
            addition = min(reach - counts[i], max(1, left * portions[i] // pool), surplus)
            counts[i] = counts[i] + addition
            surplus = surplus - addition
    return np.array(counts)


def gaussian(rng, extent, width, reach, pieces=(), kind=jnp.bfloat16):
    array = width * jax.random.normal(rng, extent, jnp.float32)
    if pieces:
        array = array * shard_levels(rng, extent, pieces, -0.22, 0.18)
    return jnp.clip(array, -reach, reach).astype(kind)


def setup_inputs(seed: int = 0, part: int = 0) -> dict:
    streams_of = jax.random.split(jax.random.key(seed), 6)
    own_keys = jax.random.split(jax.random.fold_in(streams_of[5], part), 6)
    hidden = gaussian(own_keys[0], (ROWS, HIDDEN_UNITS), 1.0, 6.0, ((0, 8), (1, 2)))
    row_adapter_index_keys = jax.random.split(jax.random.fold_in(own_keys[1], 1), ROWS // ROWS)
    row_adapter_index_turns = jax.random.permutation(jax.random.fold_in(own_keys[1], 3), ROWS // ROWS)
    row_adapter_index = jax.vmap(lambda own, number: assign_block(jax.random.fold_in(own_keys[1], 2), own, number, ROWS, ADAPTER_TOTAL, 1, CAP, 2))(row_adapter_index_keys, row_adapter_index_turns).reshape((ROWS, 1))
    down_matrix = gaussian(streams_of[2], (HIDDEN_UNITS, MODEL_WIDTH), HIDDEN_UNITS ** -0.5, 0.03125, ((0, 2), (1, 8)))
    adapter_input_factor = gaussian(streams_of[3], (ADAPTER_TOTAL, HIDDEN_UNITS, ADAPTER_RANK), HIDDEN_UNITS ** -0.5, 0.03125, ((0, 8), (1, 2)))
    adapter_output_factor = gaussian(streams_of[4], (ADAPTER_TOTAL, ADAPTER_RANK, MODEL_WIDTH), ADAPTER_RANK ** -0.5, 0.75, ((0, 8),))
    return dict(hidden=hidden, row_adapter_index=row_adapter_index, down_matrix=down_matrix, adapter_input_factor=adapter_input_factor, adapter_output_factor=adapter_output_factor)


def slot_table(row_adapter_index):
    idents = row_adapter_index[:, 0].astype(jnp.int32)
    onehot = (idents[:, None] == jnp.arange(ADAPTER_TOTAL, dtype=jnp.int32)[None, :]).astype(jnp.int32)
    running = jnp.cumsum(onehot, axis=0) - 1
    ranking = jnp.sum(onehot * running, axis=1).astype(jnp.int32)
    return idents, (idents * CAP + ranking).astype(jnp.int32)


def project_down(pair):
    return jnp.dot(pair[0], pair[1], preferred_element_type=jnp.float32)


def reference(hidden, row_adapter_index, down_matrix, adapter_input_factor, adapter_output_factor):
    idents, slots = slot_table(row_adapter_index)
    slot_range = jnp.arange(ADAPTER_TOTAL * CAP, dtype=jnp.int32)
    matches = slots[None, :] == slot_range[:, None]
    source = jnp.sum(jnp.where(matches, jnp.arange(ROWS, dtype=jnp.int32)[None, :], 0), axis=1).astype(jnp.int32)
    filled = jnp.any(matches, axis=1)
    picked = jnp.where(filled[:, None], hidden[source], jnp.zeros((), hidden.dtype)).astype(jnp.bfloat16)
    grouped_rows = picked.reshape(ADAPTER_TOTAL, CAP, HIDDEN_UNITS)
    lowrank_update = lax.map(project_down, (grouped_rows, adapter_input_factor)).astype(jnp.bfloat16)
    adapter_updates = lax.map(project_down, (lowrank_update, adapter_output_factor)).astype(jnp.bfloat16)
    delta = adapter_updates.reshape(ADAPTER_TOTAL * CAP, MODEL_WIDTH)[slots]
    base = jnp.dot(hidden, down_matrix, preferred_element_type=jnp.float32)
    return (base + delta.astype(jnp.float32)).astype(jnp.bfloat16)
```

```python
import functools

import jax
import jax.numpy as jnp
from jax import lax
from jax.experimental import pallas as pl
from jax.experimental.pallas import tpu as pltpu
from jax.sharding import PartitionSpec as P

MESH = pl.DeviceIdType.MESH
DEPTH = 1024
SKEW = 2


def fused_kernel(
    n, chunks, index_ref, hidden_ref, w_ref, a_ref, b_ref, out_ref,
    xbuf, wbuf, abuf, bbuf, acc, acc_in, low, low_in, dbuf, darr,
    w_sem, a_sem, b_sem, right_send, right_recv, left_send, left_recv,
    low_sem, acc_sem, d_send, d_recv,
):
    half = n // 2
    me = lax.axis_index("adapter")
    core = lax.axis_index("tensor")
    sibling = 1 - core
    columns = out_ref.shape[1]
    rows = out_ref.shape[0]
    capacity = dbuf.shape[1]
    parity = me % 2
    place = (1 - parity) * (me // 2) + parity * (n - 1 - me // 2)

    def at_place(p):
        p = (p + 2 * n) % n
        upper = p // half
        return (1 - upper) * 2 * p + upper * (2 * (n - 1 - p) + 1)

    right, left = at_place(place + 1), at_place(place - 1)
    from_left = [at_place(place - h) for h in range(half + 1)]
    from_right = [at_place(place + h) for h in range(half + 1)]

    def copy_right(c, h):
        block = xbuf.at[c, from_left[h - 1]]
        return pltpu.make_async_remote_copy(
            src_ref=block, dst_ref=block, send_sem=right_send.at[c, h - 1],
            recv_sem=right_recv.at[c, h - 1], device_id={"adapter": right}, device_id_type=MESH)

    def copy_left(c, h):
        block = xbuf.at[c, from_right[h - 1]]
        return pltpu.make_async_remote_copy(
            src_ref=block, dst_ref=block, send_sem=left_send.at[c, h - 1],
            recv_sem=left_recv.at[c, h - 1], device_id={"adapter": left}, device_id_type=MESH)

    def arrive_right(c, h):
        block = xbuf.at[c, from_left[h]]
        return pltpu.make_async_remote_copy(
            src_ref=block, dst_ref=block, send_sem=right_send.at[c, h - 1],
            recv_sem=right_recv.at[c, h - 1], device_id={"adapter": right}, device_id_type=MESH)

    def arrive_left(c, h):
        block = xbuf.at[c, from_right[h]]
        return pltpu.make_async_remote_copy(
            src_ref=block, dst_ref=block, send_sem=left_send.at[c, h - 1],
            recv_sem=left_recv.at[c, h - 1], device_id={"adapter": left}, device_id_type=MESH)

    barrier = pltpu.get_barrier_semaphore()
    for k in range(1, n):
        pl.semaphore_signal(
            barrier, inc=1, device_id={"adapter": (me + k) % n}, device_id_type=MESH)
    pl.semaphore_signal(barrier, inc=1, device_id={"tensor": sibling}, device_id_type=MESH)

    def w_copy(c):
        return pltpu.make_async_copy(
            w_ref.at[pl.ds(pl.multiple_of(c * DEPTH, DEPTH), DEPTH), :], wbuf.at[c], w_sem.at[c])

    def a_copy(c):
        return pltpu.make_async_copy(
            a_ref.at[0, :, pl.ds(pl.multiple_of(c * DEPTH, DEPTH), DEPTH)], abuf.at[c], a_sem.at[c])

    def b_copy(k):
        start = pl.multiple_of((2 * k + core) * columns, columns)
        return pltpu.make_async_copy(
            b_ref.at[0, :, pl.ds(start, columns)], bbuf.at[k], b_sem.at[k])

    def start_loads(c, carry):
        w_copy(c).start()
        a_copy(c).start()
        return carry

    lax.fori_loop(0, chunks, start_loads, 0)
    for k in range(n):
        b_copy(k).start()

    side = DEPTH // 2
    for c in range(chunks):
        part = hidden_ref[:, c * DEPTH:(c + 1) * DEPTH].astype(jnp.float32)
        stacked = jnp.concatenate([part[:, :side], part[:, side:]], axis=0)
        xbuf[c, me] = stacked.astype(jnp.bfloat16)
    acc[...] = jnp.zeros_like(acc)
    low[...] = jnp.zeros_like(low)

    idents = index_ref[...]
    onehot = (lax.broadcasted_iota(jnp.int32, (n, rows), 0) == idents).astype(jnp.float32)
    earlier = (
        lax.broadcasted_iota(jnp.int32, (rows, rows), 0)
        < lax.broadcasted_iota(jnp.int32, (rows, rows), 1)
    ).astype(jnp.bfloat16)
    running = jnp.dot(onehot.astype(jnp.bfloat16), earlier, preferred_element_type=jnp.float32)
    ranking = jnp.sum(onehot * running, axis=0, keepdims=True)
    slots = idents * capacity + ranking.astype(jnp.int32)
    selector = (
        lax.broadcasted_iota(jnp.int32, (capacity, rows), 0) + me * capacity == slots
    ).astype(jnp.float32).astype(jnp.bfloat16)
    placing = (
        lax.broadcasted_iota(jnp.int32, (n * capacity, rows), 0) == slots
    ).astype(jnp.float32)
    placing = placing.T.astype(jnp.bfloat16)

    pl.semaphore_wait(barrier, n)

    low_copy = pltpu.make_async_remote_copy(
        src_ref=low, dst_ref=low_in, send_sem=low_sem.at[0], recv_sem=low_sem.at[1],
        device_id={"tensor": sibling}, device_id_type=MESH)
    acc_copy = pltpu.make_async_remote_copy(
        src_ref=acc.at[sibling], dst_ref=acc_in, send_sem=acc_sem.at[0], recv_sem=acc_sem.at[1],
        device_id={"tensor": sibling}, device_id_type=MESH)

    def step(tau, carry):
        @pl.when(tau < chunks)
        def _():
            copy_right(tau, 1).start()
            copy_left(tau, 1).start()

        for h in range(1, half):
            c = tau - SKEW * h

            @pl.when((c >= 0) & (c < chunks))
            def _(c=c, h=h):
                arrive_right(c, h).wait_recv()
                if h + 1 < half:
                    copy_right(c, h + 1).start()
                else:
                    @pl.when(c % 2 == 0)
                    def _():
                        copy_right(c, h + 1).start()
                arrive_left(c, h).wait_recv()
                if h + 1 < half:
                    copy_left(c, h + 1).start()
                else:
                    @pl.when(c % 2 == 1)
                    def _():
                        copy_left(c, h + 1).start()

        c = tau - SKEW * half

        @pl.when(c >= 0)
        def _():
            @pl.when(c % 2 == 0)
            def _():
                arrive_right(c, half).wait_recv()

            @pl.when(c % 2 == 1)
            def _():
                arrive_left(c, half).wait_recv()

            a_copy(c).wait()
            w_copy(c).wait()
            pairs = xbuf[c].astype(jnp.float32).reshape(n, 2, rows // n, side)
            x = jnp.concatenate(
                [pairs[:, 0].reshape(rows, side), pairs[:, 1].reshape(rows, side)], axis=1
            ).astype(jnp.bfloat16)
            low[...] += lax.dot_general(
                x, abuf[c], (((1,), (1,)), ((), ())), preferred_element_type=jnp.float32)

            @pl.when(c == chunks - 1)
            def _():
                low_copy.start()

            for which in (sibling, core):
                start = pl.multiple_of(which * columns, columns)
                acc[which] += jnp.dot(
                    x, wbuf[c, :, pl.ds(start, columns)], preferred_element_type=jnp.float32)
                if which is sibling:
                    @pl.when(c == chunks - 1)
                    def _():
                        acc_copy.start()

        return carry

    lax.fori_loop(0, chunks + SKEW * half, step, 0)

    low_copy.wait()
    reduced = (low[...] + low_in[...]).astype(jnp.bfloat16)
    chosen = jnp.dot(selector, reduced, preferred_element_type=jnp.float32).astype(jnp.bfloat16)
    for k in range(n):
        b_copy(k).wait()

    def d_copy(k):
        return pltpu.make_async_remote_copy(
            src_ref=dbuf.at[k], dst_ref=darr.at[me], send_sem=d_send.at[k],
            recv_sem=d_recv.at[k], device_id={"adapter": (me + k) % n}, device_id_type=MESH)

    def d_arrive(k):
        return pltpu.make_async_remote_copy(
            src_ref=dbuf.at[k], dst_ref=darr.at[(me + n - k) % n], send_sem=d_send.at[k],
            recv_sem=d_recv.at[k], device_id={"adapter": (me + k) % n}, device_id_type=MESH)

    for k in range(1, n):
        dbuf[k] = jnp.dot(
            chosen, bbuf[(me + k) % n], preferred_element_type=jnp.float32
        ).astype(jnp.bfloat16)
        d_copy(k).start()
    darr[me] = jnp.dot(chosen, bbuf[me], preferred_element_type=jnp.float32).astype(jnp.bfloat16)

    acc_copy.wait()
    acc_in[...] += acc[core]
    for k in range(1, n):
        d_arrive(k).wait_recv()
    delta = jnp.dot(
        placing, darr[...].reshape(n * capacity, columns), preferred_element_type=jnp.float32)
    out_ref[...] = (acc_in[...] + delta).astype(out_ref.dtype)

    for k in range(1, n):
        d_copy(k).wait_send()

    def finish(c, carry):
        for h in range(1, half):
            copy_right(c, h).wait_send()
            copy_left(c, h).wait_send()

        @pl.when(c % 2 == 0)
        def _():
            copy_right(c, half).wait_send()

        @pl.when(c % 2 == 1)
        def _():
            copy_left(c, half).wait_send()

        return carry

    lax.fori_loop(0, chunks, finish, 0)


def fits(hidden, row_adapter_index, down_matrix, adapter_input_factor):
    n, cores = lax.axis_size("adapter"), lax.axis_size("tensor")
    count, inner, width = adapter_input_factor.shape
    columns = down_matrix.shape[1]
    return (
        n % 2 == 0 and n >= 4 and cores == 2 and count == 1 and hidden.shape[0] == 8
        and row_adapter_index.shape[0] == 8 * n and inner % DEPTH == 0
        and columns % (cores * 128) == 0 and down_matrix.size <= 16 * 1024 * 1024
    )


def fused(hidden, row_adapter_index, down_matrix, adapter_input_factor, adapter_output_factor):
    n = lax.axis_size("adapter")
    rows = row_adapter_index.shape[0]
    capacity = 2 * (rows // n)
    inner, columns = down_matrix.shape
    width = adapter_input_factor.shape[2]
    mine = columns // 2
    chunks = inner // DEPTH
    half = n // 2
    bf16, f32 = jnp.bfloat16, jnp.float32
    vmem = pl.BlockSpec(memory_space=pltpu.VMEM)
    anywhere = pl.BlockSpec(memory_space=pl.ANY)
    dma = pltpu.SemaphoreType.DMA
    return pl.pallas_call(
        functools.partial(fused_kernel, n, chunks),
        out_shape=jax.ShapeDtypeStruct((rows, mine), bf16),
        in_specs=[vmem, vmem, anywhere, anywhere, anywhere],
        out_specs=vmem,
        scratch_shapes=[
            pltpu.VMEM((chunks, n, 16, DEPTH // 2), bf16),
            pltpu.VMEM((chunks, DEPTH, columns), bf16),
            pltpu.VMEM((chunks, width, DEPTH), bf16),
            pltpu.VMEM((n, width, mine), bf16),
            pltpu.VMEM((2, rows, mine), f32),
            pltpu.VMEM((rows, mine), f32),
            pltpu.VMEM((rows, width), f32),
            pltpu.VMEM((rows, width), f32),
            pltpu.VMEM((n, capacity, mine), bf16),
            pltpu.VMEM((n, capacity, mine), bf16),
            dma((chunks,)), dma((chunks,)), dma((n,)),
            dma((chunks, half)), dma((chunks, half)), dma((chunks, half)), dma((chunks, half)),
            dma((2,)), dma((2,)), dma((n,)), dma((n,)),
        ],
        compiler_params=pltpu.CompilerParams(
            collective_id=0, has_side_effects=True, vmem_limit_bytes=56 * 1024 * 1024),
        cost_estimate=pl.CostEstimate(
            flops=2 * rows * inner * (columns + width),
            bytes_accessed=2 * inner * (columns + width), transcendentals=0),
    )(
        row_adapter_index.reshape(1, rows), hidden, down_matrix,
        jnp.swapaxes(adapter_input_factor, 1, 2), adapter_output_factor,
    )


def slot_table(row_adapter_index, capacity, adapters):
    idents = row_adapter_index[:, 0]
    onehot = (idents[:, None] == jnp.arange(adapters, dtype=jnp.int32)[None, :]).astype(jnp.int32)
    running = jnp.cumsum(onehot, axis=0) - 1
    ranking = jnp.sum(onehot * running, axis=1)
    return (idents, idents * capacity + ranking)


def on_device(hidden, row_adapter_index, down_matrix, adapter_input_factor, adapter_output_factor):
    adapter_count = lax.axis_size("adapter")
    tensor_count = lax.axis_size("tensor")
    if fits(hidden, row_adapter_index, down_matrix, adapter_input_factor):
        return fused(
            hidden, row_adapter_index, down_matrix, adapter_input_factor, adapter_output_factor)
    local_row_count, inner_product, adapter_rank_width = adapter_input_factor.shape
    adapters = local_row_count * adapter_count
    rows_total = row_adapter_index.shape[0]
    capacity = 2 * (rows_total // adapter_count) // local_row_count
    idents, slots = slot_table(row_adapter_index, capacity, adapters)
    own_slots = local_row_count * capacity
    first = lax.axis_index("adapter") * own_slots
    wanted = first + jnp.arange(own_slots, dtype=jnp.int32)
    selector = (slots[None, :] == wanted[:, None]).astype(jnp.bfloat16)
    columns = down_matrix.shape[1]
    piece = lax.all_gather(hidden, "adapter", axis=0, tiled=True)
    product = jnp.dot(piece, down_matrix, preferred_element_type=jnp.float32)
    picked = jnp.dot(selector, piece, preferred_element_type=jnp.float32)
    selected_rows = picked.astype(jnp.bfloat16).reshape(local_row_count, capacity, inner_product)
    partial_rank = jnp.einsum(
        "ldm,lmu->ldu", selected_rows, adapter_input_factor, preferred_element_type=jnp.float32
    )
    reduced = lax.psum(partial_rank, "tensor").astype(jnp.bfloat16)
    narrow_hidden = columns // tensor_count
    part_index = lax.axis_index("tensor")
    output_factor_split = adapter_output_factor.reshape(
        local_row_count, adapter_rank_width, adapter_count, tensor_count, narrow_hidden
    )
    b_mine = lax.dynamic_slice_in_dim(output_factor_split, part_index, 1, 3)[:, :, :, 0, :]
    produced = jnp.einsum(
        "ask,akjc->jasc", reduced, b_mine, preferred_element_type=jnp.float32
    ).astype(jnp.bfloat16)
    produced = produced.reshape(adapter_count, own_slots * narrow_hidden)
    arrived = lax.all_to_all(produced, "adapter", split_axis=0, concat_axis=0, tiled=True).reshape(
        adapters * capacity, narrow_hidden
    )
    delta = jnp.take(arrived, slots, axis=0)
    summed = lax.psum_scatter(product, "tensor", scatter_dimension=1, tiled=True)
    return (summed + delta.astype(jnp.float32)).astype(jnp.bfloat16)


def solution(mesh):
    in_specs = (
        P(("groups", "adapter"), "tensor"),
        P("groups", None),
        P("tensor", "adapter"),
        P("adapter", "tensor", None),
        P("adapter", None, None),
    )
    out_specs = P("groups", ("adapter", "tensor"))
    return jax.shard_map(
        on_device, mesh=mesh, in_specs=in_specs, out_specs=out_specs, check_vma=False
    )
```

```python
import functools

import jax
import jax.numpy as jnp
from jax import lax
from jax.experimental import pallas as pl
from jax.experimental.pallas import tpu as pltpu
from jax.sharding import PartitionSpec as P

MESH = pl.DeviceIdType.MESH
DEPTH = 3584
SKEW = 2


def fused_kernel(
    n, chunks, index_hbm, hidden_hbm, w_ref, a_ref, b_ref, out_ref,
    hidden_ref, index_ref, xbuf, wbuf, abuf, bbuf, acc, acc_in, low, low_in, dbuf, darr,
    w_sem, a_sem, b_sem, right_send, right_recv, left_send, left_recv,
    low_sem, acc_sem, d_send, d_recv, in_sem,
):
    half = n // 2
    me = lax.axis_index("adapter")
    core = lax.axis_index("tensor")
    sibling = 1 - core
    columns = out_ref.shape[1]
    rows = out_ref.shape[0]
    capacity = dbuf.shape[1]
    parity = me % 2
    place = (1 - parity) * (me // 2) + parity * (n - 1 - me // 2)

    def at_place(p):
        p = (p + 2 * n) % n
        upper = p // half
        return (1 - upper) * 2 * p + upper * (2 * (n - 1 - p) + 1)

    right, left = at_place(place + 1), at_place(place - 1)
    from_left = [at_place(place - h) for h in range(half + 1)]
    from_right = [at_place(place + h) for h in range(half + 1)]

    def copy_right(c, h):
        block = xbuf.at[c, from_left[h - 1]]
        return pltpu.make_async_remote_copy(
            src_ref=block, dst_ref=block, send_sem=right_send.at[c, h - 1],
            recv_sem=right_recv.at[c, h - 1], device_id={"adapter": right}, device_id_type=MESH)

    def copy_left(c, h):
        block = xbuf.at[c, from_right[h - 1]]
        return pltpu.make_async_remote_copy(
            src_ref=block, dst_ref=block, send_sem=left_send.at[c, h - 1],
            recv_sem=left_recv.at[c, h - 1], device_id={"adapter": left}, device_id_type=MESH)

    def arrive_right(c, h):
        block = xbuf.at[c, from_left[h]]
        return pltpu.make_async_remote_copy(
            src_ref=block, dst_ref=block, send_sem=right_send.at[c, h - 1],
            recv_sem=right_recv.at[c, h - 1], device_id={"adapter": right}, device_id_type=MESH)

    def arrive_left(c, h):
        block = xbuf.at[c, from_right[h]]
        return pltpu.make_async_remote_copy(
            src_ref=block, dst_ref=block, send_sem=left_send.at[c, h - 1],
            recv_sem=left_recv.at[c, h - 1], device_id={"adapter": left}, device_id_type=MESH)

    barrier = pltpu.get_barrier_semaphore()
    for k in range(1, n):
        pl.semaphore_signal(
            barrier, inc=1, device_id={"adapter": (me + k) % n}, device_id_type=MESH)
    pl.semaphore_signal(barrier, inc=1, device_id={"tensor": sibling}, device_id_type=MESH)

    def w_copy(c):
        return pltpu.make_async_copy(
            w_ref.at[pl.ds(pl.multiple_of(c * DEPTH, DEPTH), DEPTH), :], wbuf.at[c], w_sem.at[c])

    def a_copy(c):
        return pltpu.make_async_copy(
            a_ref.at[0, :, pl.ds(pl.multiple_of(c * DEPTH, DEPTH), DEPTH)], abuf.at[c], a_sem.at[c])

    def b_copy(k):
        start = pl.multiple_of((2 * k + core) * columns, columns)
        return pltpu.make_async_copy(
            b_ref.at[0, :, pl.ds(start, columns)], bbuf.at[k], b_sem.at[k])

    hidden_copy = pltpu.make_async_copy(hidden_hbm, hidden_ref, in_sem.at[0])
    index_copy = pltpu.make_async_copy(index_hbm, index_ref, in_sem.at[1])
    hidden_copy.start()
    index_copy.start()
    hidden_copy.wait()

    side = DEPTH // 2
    for c in range(chunks):
        part = hidden_ref[:, c * DEPTH:(c + 1) * DEPTH].astype(jnp.float32)
        stacked = jnp.concatenate([part[:, :side], part[:, side:]], axis=0)
        xbuf[c, me] = stacked.astype(jnp.bfloat16)

    pl.semaphore_wait(barrier, n)
    for c in range(SKEW):
        copy_right(c, 1).start()
        copy_left(c, 1).start()

    def start_loads(c, carry):
        w_copy(c).start()
        a_copy(c).start()
        return carry

    lax.fori_loop(0, chunks, start_loads, 0)
    for k in range(n):
        b_copy(k).start()

    acc[...] = jnp.zeros_like(acc)
    low[...] = jnp.zeros_like(low)

    index_copy.wait()
    idents = index_ref[...]
    onehot = (lax.broadcasted_iota(jnp.int32, (n, rows), 0) == idents).astype(jnp.float32)
    earlier = (
        lax.broadcasted_iota(jnp.int32, (rows, rows), 0)
        < lax.broadcasted_iota(jnp.int32, (rows, rows), 1)
    ).astype(jnp.bfloat16)
    running = jnp.dot(onehot.astype(jnp.bfloat16), earlier, preferred_element_type=jnp.float32)
    ranking = jnp.sum(onehot * running, axis=0, keepdims=True)
    slots = idents * capacity + ranking.astype(jnp.int32)
    selector = (
        lax.broadcasted_iota(jnp.int32, (capacity, rows), 0) + me * capacity == slots
    ).astype(jnp.float32).astype(jnp.bfloat16)
    placing = (
        lax.broadcasted_iota(jnp.int32, (n * capacity, rows), 0) == slots
    ).astype(jnp.float32)
    placing = placing.T.astype(jnp.bfloat16)

    low_copy = pltpu.make_async_remote_copy(
        src_ref=low, dst_ref=low_in, send_sem=low_sem.at[0], recv_sem=low_sem.at[1],
        device_id={"tensor": sibling}, device_id_type=MESH)
    acc_copy = pltpu.make_async_remote_copy(
        src_ref=acc.at[sibling], dst_ref=acc_in, send_sem=acc_sem.at[0], recv_sem=acc_sem.at[1],
        device_id={"tensor": sibling}, device_id_type=MESH)

    def step(tau, carry):
        @pl.when(tau < chunks)
        def _():
            copy_right(tau, 1).start()
            copy_left(tau, 1).start()

        for h in range(1, half):
            c = tau - SKEW * h

            @pl.when((c >= 0) & (c < chunks))
            def _(c=c, h=h):
                arrive_right(c, h).wait_recv()
                if h + 1 < half:
                    copy_right(c, h + 1).start()
                else:
                    @pl.when(c % 2 == 0)
                    def _():
                        copy_right(c, h + 1).start()
                arrive_left(c, h).wait_recv()
                if h + 1 < half:
                    copy_left(c, h + 1).start()
                else:
                    @pl.when(c % 2 == 1)
                    def _():
                        copy_left(c, h + 1).start()

        c = tau - SKEW * half

        @pl.when(c >= 0)
        def _():
            @pl.when(c % 2 == 0)
            def _():
                arrive_right(c, half).wait_recv()

            @pl.when(c % 2 == 1)
            def _():
                arrive_left(c, half).wait_recv()

            a_copy(c).wait()
            w_copy(c).wait()
            pairs = xbuf[c].astype(jnp.float32).reshape(n, 2, rows // n, side)
            x = jnp.concatenate(
                [pairs[:, 0].reshape(rows, side), pairs[:, 1].reshape(rows, side)], axis=1
            ).astype(jnp.bfloat16)
            low[...] += lax.dot_general(
                x, abuf[c], (((1,), (1,)), ((), ())), preferred_element_type=jnp.float32)

            @pl.when(c == chunks - 1)
            def _():
                low_copy.start()

            for which in (sibling, core):
                start = pl.multiple_of(which * columns, columns)
                acc[which] += jnp.dot(
                    x, wbuf[c, :, pl.ds(start, columns)], preferred_element_type=jnp.float32)
                if which is sibling:
                    @pl.when(c == chunks - 1)
                    def _():
                        acc_copy.start()

        return carry

    lax.fori_loop(SKEW, chunks + SKEW * half, step, 0)

    low_copy.wait()
    reduced = (low[...] + low_in[...]).astype(jnp.bfloat16)
    chosen = jnp.dot(selector, reduced, preferred_element_type=jnp.float32).astype(jnp.bfloat16)
    for k in range(n):
        b_copy(k).wait()

    def d_copy(k):
        return pltpu.make_async_remote_copy(
            src_ref=dbuf.at[k], dst_ref=darr.at[me], send_sem=d_send.at[k],
            recv_sem=d_recv.at[k], device_id={"adapter": (me + k) % n}, device_id_type=MESH)

    def d_arrive(k):
        return pltpu.make_async_remote_copy(
            src_ref=dbuf.at[k], dst_ref=darr.at[(me + n - k) % n], send_sem=d_send.at[k],
            recv_sem=d_recv.at[k], device_id={"adapter": (me + k) % n}, device_id_type=MESH)

    for k in sorted(range(1, n), key=lambda k: -min(k, n - k)):
        dbuf[k] = jnp.dot(
            chosen, bbuf[(me + k) % n], preferred_element_type=jnp.float32
        ).astype(jnp.bfloat16)
        d_copy(k).start()
    darr[me] = jnp.dot(chosen, bbuf[me], preferred_element_type=jnp.float32).astype(jnp.bfloat16)

    acc_copy.wait()
    acc_in[...] += acc[core]
    for k in range(1, n):
        d_arrive(k).wait_recv()
    delta = jnp.dot(
        placing, darr[...].reshape(n * capacity, columns), preferred_element_type=jnp.float32)
    out_ref[...] = (acc_in[...] + delta).astype(out_ref.dtype)

    for k in range(1, n):
        d_copy(k).wait_send()

    def finish(c, carry):
        for h in range(1, half):
            copy_right(c, h).wait_send()
            copy_left(c, h).wait_send()

        @pl.when(c % 2 == 0)
        def _():
            copy_right(c, half).wait_send()

        @pl.when(c % 2 == 1)
        def _():
            copy_left(c, half).wait_send()

        return carry

    lax.fori_loop(0, chunks, finish, 0)


def fits(hidden, row_adapter_index, down_matrix, adapter_input_factor):
    n, cores = lax.axis_size("adapter"), lax.axis_size("tensor")
    count, inner, width = adapter_input_factor.shape
    columns = down_matrix.shape[1]
    return (
        n % 2 == 0 and n >= 4 and cores == 2 and count == 1 and hidden.shape[0] == 8
        and row_adapter_index.shape[0] == 8 * n and inner % DEPTH == 0
        and columns % (cores * 128) == 0 and down_matrix.size <= 16 * 1024 * 1024
    )


def fused(hidden, row_adapter_index, down_matrix, adapter_input_factor, adapter_output_factor):
    n = lax.axis_size("adapter")
    rows = row_adapter_index.shape[0]
    capacity = 2 * (rows // n)
    inner, columns = down_matrix.shape
    width = adapter_input_factor.shape[2]
    mine = columns // 2
    chunks = inner // DEPTH
    half = n // 2
    bf16, f32 = jnp.bfloat16, jnp.float32
    vmem = pl.BlockSpec(memory_space=pltpu.VMEM)
    anywhere = pl.BlockSpec(memory_space=pl.ANY)
    dma = pltpu.SemaphoreType.DMA
    return pl.pallas_call(
        functools.partial(fused_kernel, n, chunks),
        out_shape=jax.ShapeDtypeStruct((rows, mine), bf16),
        in_specs=[anywhere] * 5,
        out_specs=vmem,
        scratch_shapes=[
            pltpu.VMEM(hidden.shape, bf16),
            pltpu.VMEM((1, rows), jnp.int32),
            pltpu.VMEM((chunks, n, 16, DEPTH // 2), bf16),
            pltpu.VMEM((chunks, DEPTH, columns), bf16),
            pltpu.VMEM((chunks, width, DEPTH), bf16),
            pltpu.VMEM((n, width, mine), bf16),
            pltpu.VMEM((2, rows, mine), f32),
            pltpu.VMEM((rows, mine), f32),
            pltpu.VMEM((rows, width), f32),
            pltpu.VMEM((rows, width), f32),
            pltpu.VMEM((n, capacity, mine), bf16),
            pltpu.VMEM((n, capacity, mine), bf16),
            dma((chunks,)), dma((chunks,)), dma((n,)),
            dma((chunks, half)), dma((chunks, half)), dma((chunks, half)), dma((chunks, half)),
            dma((2,)), dma((2,)), dma((n,)), dma((n,)), dma((2,)),
        ],
        compiler_params=pltpu.CompilerParams(
            collective_id=0, has_side_effects=True, vmem_limit_bytes=56 * 1024 * 1024),
        cost_estimate=pl.CostEstimate(
            flops=2 * rows * inner * (columns + width),
            bytes_accessed=2 * inner * (columns + width), transcendentals=0),
    )(
        row_adapter_index.reshape(1, rows), hidden, down_matrix,
        jnp.swapaxes(adapter_input_factor, 1, 2), adapter_output_factor,
    )


def slot_table(row_adapter_index, capacity, adapters):
    idents = row_adapter_index[:, 0]
    onehot = (idents[:, None] == jnp.arange(adapters, dtype=jnp.int32)[None, :]).astype(jnp.int32)
    running = jnp.cumsum(onehot, axis=0) - 1
    ranking = jnp.sum(onehot * running, axis=1)
    return (idents, idents * capacity + ranking)


def on_device(hidden, row_adapter_index, down_matrix, adapter_input_factor, adapter_output_factor):
    adapter_count = lax.axis_size("adapter")
    tensor_count = lax.axis_size("tensor")
    if fits(hidden, row_adapter_index, down_matrix, adapter_input_factor):
        return fused(
            hidden, row_adapter_index, down_matrix, adapter_input_factor, adapter_output_factor)
    local_row_count, inner_product, adapter_rank_width = adapter_input_factor.shape
    adapters = local_row_count * adapter_count
    rows_total = row_adapter_index.shape[0]
    capacity = 2 * (rows_total // adapter_count) // local_row_count
    idents, slots = slot_table(row_adapter_index, capacity, adapters)
    own_slots = local_row_count * capacity
    first = lax.axis_index("adapter") * own_slots
    wanted = first + jnp.arange(own_slots, dtype=jnp.int32)
    selector = (slots[None, :] == wanted[:, None]).astype(jnp.bfloat16)
    columns = down_matrix.shape[1]
    piece = lax.all_gather(hidden, "adapter", axis=0, tiled=True)
    product = jnp.dot(piece, down_matrix, preferred_element_type=jnp.float32)
    picked = jnp.dot(selector, piece, preferred_element_type=jnp.float32)
    selected_rows = picked.astype(jnp.bfloat16).reshape(local_row_count, capacity, inner_product)
    partial_rank = jnp.einsum(
        "ldm,lmu->ldu", selected_rows, adapter_input_factor, preferred_element_type=jnp.float32
    )
    reduced = lax.psum(partial_rank, "tensor").astype(jnp.bfloat16)
    narrow_hidden = columns // tensor_count
    part_index = lax.axis_index("tensor")
    output_factor_split = adapter_output_factor.reshape(
        local_row_count, adapter_rank_width, adapter_count, tensor_count, narrow_hidden
    )
    b_mine = lax.dynamic_slice_in_dim(output_factor_split, part_index, 1, 3)[:, :, :, 0, :]
    produced = jnp.einsum(
        "ask,akjc->jasc", reduced, b_mine, preferred_element_type=jnp.float32
    ).astype(jnp.bfloat16)
    produced = produced.reshape(adapter_count, own_slots * narrow_hidden)
    arrived = lax.all_to_all(produced, "adapter", split_axis=0, concat_axis=0, tiled=True).reshape(
        adapters * capacity, narrow_hidden
    )
    delta = jnp.take(arrived, slots, axis=0)
    summed = lax.psum_scatter(product, "tensor", scatter_dimension=1, tiled=True)
    return (summed + delta.astype(jnp.float32)).astype(jnp.bfloat16)


def solution(mesh):
    in_specs = (
        P(("groups", "adapter"), "tensor"),
        P("groups", None),
        P("tensor", "adapter"),
        P("adapter", "tensor", None),
        P("adapter", None, None),
    )
    out_specs = P("groups", ("adapter", "tensor"))
    return jax.shard_map(
        on_device, mesh=mesh, in_specs=in_specs, out_specs=out_specs, check_vma=False
    )
```
